32 devices in a mesh: row: 8 (over z, y), col: 4 (over x, core).
Axes of the slice: x: 2, y: 2, z: 4, core: 2. Of those that a mesh axis runs over, the one named last changes fastest.
Arguments:
- coeff: bfloat16 [3072, 1536], P('row', 'col'), may hold values from -6 to 6
- bank: bfloat16 [16, 384, 384], replicated, may hold values from -0.09375 to 0.09375
- alpha_tiles: int32 [8, 24], replicated, may hold values from 0 to 7
- alpha_blocks: int32 [8, 24], replicated, may hold values from 0 to 15
- alpha_count: int32 [8], replicated, may hold values from 2 to 24, as said below
- beta_tiles: int32 [4, 24], replicated, may hold values from 0 to 3
- beta_blocks: int32 [4, 24], replicated, may hold values from 0 to 15
- beta_count: int32 [4], replicated, may hold values from 2 to 24, as said below
Outputs:
- sigma: float32 [3072, 1536], P('row', 'col')
The draws below stay inside these ranges and needn't reach their ends.
Inputs may be any that keep to these rules, and one draw needn't show every extreme that they name: `alpha_count`: every value lies in 2 to 24; some tile has all 24 slots live. `beta_count`: every value lies in 2 to 24; some tile has all 24 slots live.
All inputs are finite; a program needn't handle non-finite values.
Results may differ from the reference program's by a relative error of at most 0.0003.
Values may be sent and summed in bfloat16 or wider, within the bound.
A program may use at most 64 MiB of HBM per device.

```python
import jax
import jax.numpy as jnp
from jax import lax

TILE = 384
LIST = 24
BANK = 16
NA = 3072
NB = 1536
N_ROW = 8
N_COL = 4


def draw_alpha_count(key, part):
    values = jax.random.randint(jax.random.fold_in(key, 11), (N_ROW,), 2, LIST + 1)
    chosen = jax.random.randint(jax.random.fold_in(key, 12), (), 0, N_ROW)
    return values.at[chosen].set(LIST).astype(jnp.int32)


def draw_beta_count(key, part):
    values = jax.random.randint(jax.random.fold_in(key, 21), (N_COL,), 2, LIST + 1)
    chosen = jax.random.randint(jax.random.fold_in(key, 22), (), 0, N_COL)
    return values.at[chosen].set(LIST).astype(jnp.int32)


def set_ends(values, key, smallest, high):
    longest = values.shape.index(max(values.shape))
    spots = []
    for shift in (0, 1):
        where = [jax.random.randint(jax.random.fold_in(key, axis), (), 0, length) for axis, length in enumerate(values.shape)]
        where[longest] = (where[longest] + shift) % values.shape[longest]
        spots.append(tuple(where))
    return values.at[spots[0]].set(smallest).at[spots[1]].set(high)


def block_levels(rng, extent, pieces, smallest, largest):
    level = 1.0
    for dim, parts in pieces:
        steps = jax.random.uniform(jax.random.fold_in(jax.random.fold_in(rng, 6), dim), (parts,), jnp.float32, smallest / len(pieces), largest / len(pieces))
        level = level * jnp.repeat(jnp.exp(steps), extent[dim] // parts).reshape((-1,) + (1,) * (len(extent) - 1 - dim))
    return level


def noise(stream_key, shape, scale, limit, pieces=(), kind=jnp.bfloat16):
    drawn = scale * jax.random.normal(stream_key, shape, jnp.float32)
    if pieces:
        drawn = drawn * block_levels(stream_key, shape, pieces, -0.22, 0.18)
    return jnp.clip(drawn, -limit, limit).astype(kind)


def setup_inputs(seed: int = 0) -> dict:
    splits = jax.random.split(jax.random.key(seed), 9)
    return {
        "coeff": noise(splits[0], (NA, NB), 1.0, 6.0, ((0, 8), (1, 4))),
        "bank": noise(splits[1], (BANK, TILE, TILE), (TILE * LIST // 2) ** -0.5, 0.09375),
        "alpha_tiles": set_ends(jax.random.randint(splits[2], (N_ROW, LIST), 0, N_ROW), jax.random.fold_in(splits[2], 1), 0, N_ROW - 1).astype(jnp.int32),
        "alpha_blocks": set_ends(jax.random.randint(splits[3], (N_ROW, LIST), 0, BANK), jax.random.fold_in(splits[3], 1), 0, BANK - 1).astype(jnp.int32),
        "alpha_count": draw_alpha_count(jax.random.fold_in(splits[8], 71), 0),
        "beta_tiles": set_ends(jax.random.randint(splits[5], (N_COL, LIST), 0, N_COL), jax.random.fold_in(splits[5], 1), 0, N_COL - 1).astype(jnp.int32),
        "beta_blocks": set_ends(jax.random.randint(splits[6], (N_COL, LIST), 0, BANK), jax.random.fold_in(splits[6], 1), 0, BANK - 1).astype(jnp.int32),
        "beta_count": draw_beta_count(jax.random.fold_in(splits[8], 71), 0),
    }


def reference(coeff, bank, alpha_tiles, alpha_blocks, alpha_count, beta_tiles, beta_blocks, beta_count):
    def alpha_rows(tile_row):
        tiles = alpha_tiles[tile_row]
        blocks = alpha_blocks[tile_row]

        def add_slot(slot, total):
            start = (tiles[slot] * TILE).astype(jnp.int32)
            piece = lax.dynamic_slice_in_dim(coeff, start, TILE, 0)
            return total + jnp.dot(bank[blocks[slot]], piece, preferred_element_type=jnp.float32)

        return lax.fori_loop(0, alpha_count[tile_row], add_slot, jnp.zeros((TILE, NB), jnp.float32))

    def beta_cols(tile_col):
        tiles = beta_tiles[tile_col]
        blocks = beta_blocks[tile_col]

        def add_slot(slot, total):
            start = (tiles[slot] * TILE).astype(jnp.int32)
            piece = lax.dynamic_slice_in_dim(coeff, start, TILE, 1)
            return total + lax.dot_general(piece, bank[blocks[slot]], (((1,), (1,)), ((), ())), preferred_element_type=jnp.float32)

        return lax.fori_loop(0, beta_count[tile_col], add_slot, jnp.zeros((NA, TILE), jnp.float32))

    sigma_alpha = lax.map(alpha_rows, jnp.arange(N_ROW, dtype=jnp.int32)).reshape(NA, NB)
    sigma_beta = lax.map(beta_cols, jnp.arange(N_COL, dtype=jnp.int32))
    sigma_beta = jnp.transpose(sigma_beta, (1, 0, 2)).reshape(NA, NB)
    return sigma_alpha + sigma_beta
```

```python
import functools

import jax
import jax.numpy as jnp
from jax import lax
from jax.experimental import pallas as pl
from jax.experimental.pallas import tpu as pltpu
from jax.sharding import PartitionSpec as P

MESH = pl.DeviceIdType.MESH
LATE = 1


def kernel(
    n_row, n_col,
    a_tiles, a_blocks, a_count, b_tiles, b_blocks, b_count,
    coeff, bank_hbm, out,
    rows, cols, bank, local_sem, row_send, row_recv, col_send, col_recv,
):
    tile = coeff.shape[0]
    half = tile // 2
    slots = a_tiles.shape[1]
    depth, width = n_row // 2, n_col // 2
    row, col = lax.axis_index("row"), lax.axis_index("col")
    z, y = row // 2, row % 2
    x, core = col // 2, col % 2
    mate = row + 1 - 2 * y
    twin = col + 1 - 2 * core

    def part(ref, which, h):
        return ref.at[which, pl.ds(h * half, half), :]

    def own(h):
        return coeff.at[pl.ds(h * half, half), :]

    def row_copy(src, which, h, way, target):
        return pltpu.make_async_remote_copy(
            src_ref=src, dst_ref=part(rows, which, h),
            send_sem=row_send.at[way, which, h], recv_sem=row_recv.at[which, h],
            device_id=(target, col), device_id_type=MESH,
        )

    def col_copy(src, which, h, way, target):
        return pltpu.make_async_remote_copy(
            src_ref=src, dst_ref=part(cols, which, h),
            send_sem=col_send.at[way, which, h], recv_sem=col_recv.at[which, h],
            device_id=(row, target), device_id_type=MESH,
        )

    def arrived(which, h):
        row_copy(own(h), which, h, 0, mate).wait_recv()

    bank_copy = pltpu.make_async_copy(bank_hbm, bank, local_sem.at[0])
    bank_copy.start()
    own_row = pltpu.make_async_copy(coeff, rows.at[row], local_sem.at[1])
    own_row.start()
    own_col = pltpu.make_async_copy(coeff, cols.at[col], local_sem.at[2])
    own_col.start()

    has_up, has_down = z + 1 < depth, z >= 1

    barrier = pltpu.get_barrier_semaphore()

    def greet(r, c):
        pl.semaphore_signal(barrier, inc=1, device_id=(r, c), device_id_type=MESH)

    @pl.when(has_up)
    def _():
        greet(row + 2, col)

    @pl.when(has_down)
    def _():
        greet(row - 2, col)

    greet(mate, col)
    greet(row, twin)
    for step in range(1, width):
        greet(row, lax.rem(x + step, width) * 2 + core)
    neighbours = 1 + width + has_up.astype(jnp.int32) + has_down.astype(jnp.int32)
    pl.semaphore_wait(barrier, neighbours)

    UP, DOWN, SIDE = 0, 1, 2

    for h in (0, 1):
        @pl.when(has_up)
        def _():
            row_copy(own(h), row, h, UP, row + 2).start()

        @pl.when(has_down)
        def _():
            row_copy(own(h), row, h, DOWN, row - 2).start()

        row_copy(own(h), row, h, SIDE, mate).start()
        for step in range(1, width):
            col_copy(own(h), col, h, step, lax.rem(x + step, width) * 2 + core).start()
        col_copy(own(h), col, h, 0, twin).start()

    def pass_rows(d, h):
        below, above = row - 2 * d, row + 2 * d

        @pl.when(z >= d)
        def _():
            arrived(below, h)

            @pl.when(has_up)
            def _():
                row_copy(part(rows, below, h), below, h, UP, row + 2).start()

            if d != 1 or h != LATE:
                row_copy(part(rows, below, h), below, h, SIDE, mate).start()

        @pl.when(z + d < depth)
        def _():
            arrived(above, h)

            @pl.when(has_down)
            def _():
                row_copy(part(rows, above, h), above, h, DOWN, row - 2).start()

            if d != 1 or h != LATE:
                row_copy(part(rows, above, h), above, h, SIDE, mate).start()

    def pass_mate():
        arrived(mate, LATE)

        @pl.when(has_up)
        def _():
            row_copy(part(rows, mate, LATE), mate, LATE, UP, row + 2).start()

        @pl.when(has_down)
        def _():
            row_copy(part(rows, mate, LATE), mate, LATE, DOWN, row - 2).start()

    def pass_cols(h):
        for step in range(1, width):
            source = lax.rem(x + width - step, width) * 2 + core
            col_copy(own(h), source, h, 0, twin).wait_recv()
            col_copy(part(cols, source, h), source, h, 0, twin).start()

    pass_rows(1, 0)
    pass_cols(0)
    pass_rows(1, 1)
    pass_cols(1)
    if depth > 2:
        pass_rows(2, 0)

    own_col.wait()
    bank_copy.wait()
    for h in (0, 1):
        for step in range(width):
            source = lax.rem(x + step, width) * 2 + 1 - core
            col_copy(own(h), source, h, 0, twin).wait_recv()
    out[...] = jnp.zeros_like(out)
    b_live = b_count[col]

    def add_beta(slot):
        piece = cols[b_tiles[col, slot]]
        block = bank[b_blocks[col, slot]]
        live = jnp.where(slot < b_live, 1.0, 0.0).astype(jnp.float32)
        out[...] += live * lax.dot_general(
            piece, block, (((1,), (1,)), ((), ())), preferred_element_type=jnp.float32
        )

    def beta_range(low, high):
        def body(slot, carry):
            add_beta(slot)
            return carry
        lax.fori_loop(low, high, body, 0)

    beta_range(0, slots // 3)
    if depth > 2:
        pass_rows(2, 1)
    else:
        pass_mate()
    beta_range(slots // 3, 2 * slots // 3)
    if depth > 2:
        pass_mate()
    for d in range(3, depth):
        pass_rows(d, 0)
        if d == 3:
            beta_range(2 * slots // 3, slots)
        pass_rows(d, 1)
    if depth <= 3:
        beta_range(2 * slots // 3, slots)

    own_row.wait()
    arrived(mate, 1 - LATE)
    for d in range(1, depth):
        for h in (0, 1):
            @pl.when(z >= d)
            def _():
                arrived(mate - 2 * d, h)

            @pl.when(z + d < depth)
            def _():
                arrived(mate + 2 * d, h)

    a_live = a_count[row]

    def add_alpha(slot, carry):
        piece = rows[a_tiles[row, slot]]
        block = bank[a_blocks[row, slot]]
        live = jnp.where(slot < a_live, 1.0, 0.0).astype(jnp.float32)
        out[...] += live * jnp.dot(block, piece, preferred_element_type=jnp.float32)
        return carry

    lax.fori_loop(0, slots, add_alpha, 0)

    def sent_row(which, h, way):
        row_copy(own(h), which, h, way, mate).wait_send()

    for h in (0, 1):
        @pl.when(has_up)
        def _():
            sent_row(row, h, UP)

        @pl.when(has_down)
        def _():
            sent_row(row, h, DOWN)

        sent_row(row, h, SIDE)
        for step in range(1, width):
            col_copy(own(h), col, h, step, twin).wait_send()
        for step in range(width):
            source = lax.rem(x + step, width) * 2 + core
            col_copy(own(h), source, h, 0, twin).wait_send()
        for d in range(1, depth):
            @pl.when(z >= d)
            def _():
                @pl.when(has_up)
                def _():
                    sent_row(row - 2 * d, h, UP)

                if d != 1 or h != LATE:
                    sent_row(row - 2 * d, h, SIDE)

            @pl.when(z + d < depth)
            def _():
                @pl.when(has_down)
                def _():
                    sent_row(row + 2 * d, h, DOWN)

                if d != 1 or h != LATE:
                    sent_row(row + 2 * d, h, SIDE)

    @pl.when(has_up)
    def _():
        sent_row(mate, LATE, UP)

    @pl.when(has_down)
    def _():
        sent_row(mate, LATE, DOWN)


def solution(mesh):
    n_row, n_col = mesh.shape["row"], mesh.shape["col"]

    def local(coeff, bank, a_tiles, a_blocks, a_count, b_tiles, b_blocks, b_count):
        tile = coeff.shape[0]
        flops = 2 * (a_tiles.shape[1] + b_tiles.shape[1]) * tile**3
        return pl.pallas_call(
            functools.partial(kernel, n_row, n_col),
            out_shape=jax.ShapeDtypeStruct((tile, tile), jnp.float32),
            in_specs=[pl.BlockSpec(memory_space=pltpu.SMEM)] * 6
            + [pl.BlockSpec(memory_space=pltpu.HBM)] * 2,
            out_specs=pl.BlockSpec(memory_space=pltpu.VMEM),
            scratch_shapes=[
                pltpu.VMEM((n_row, tile, tile), coeff.dtype),
                pltpu.VMEM((n_col, tile, tile), coeff.dtype),
                pltpu.VMEM(bank.shape, bank.dtype),
                pltpu.SemaphoreType.DMA((3,)),
                pltpu.SemaphoreType.DMA((3, n_row, 2)),
                pltpu.SemaphoreType.DMA((n_row, 2)),
                pltpu.SemaphoreType.DMA((max(1, n_col // 2), n_col, 2)),
                pltpu.SemaphoreType.DMA((n_col, 2)),
            ],
            compiler_params=pltpu.CompilerParams(
                collective_id=0, has_side_effects=True, vmem_limit_bytes=62 * 1024 * 1024
            ),
            cost_estimate=pl.CostEstimate(
                flops=flops, bytes_accessed=bank.size * 2 + tile * tile * 6, transcendentals=0
            ),
        )(a_tiles, a_blocks, a_count, b_tiles, b_blocks, b_count, coeff, bank)

    return jax.shard_map(
        local,
        mesh=mesh,
        in_specs=(P("row", "col"), P(), P(), P(), P(), P(), P(), P()),
        out_specs=P("row", "col"),
        check_vma=False,
    )
```

```python
import functools

import jax
import jax.numpy as jnp
from jax import lax
from jax.experimental import pallas as pl
from jax.experimental.pallas import tpu as pltpu
from jax.sharding import PartitionSpec as P

MESH = pl.DeviceIdType.MESH
LATE = 1


GROUP = 4
STRIP = 16


def counted(tiles, blocks, place, count, n_bank, into):
    code = tiles[pl.ds(place, 1), :] * n_bank + blocks[pl.ds(place, 1), :]
    slot = lax.broadcasted_iota(jnp.int32, code.shape, 1)
    code = jnp.where(slot < count, code, -1)
    shape = (into.shape[0], code.shape[1])
    hit = lax.broadcasted_iota(jnp.int32, shape, 0) == code
    times = jnp.sum(jnp.where(hit, 1.0, 0.0).astype(jnp.float32), axis=1, keepdims=True)
    into[...] = jnp.broadcast_to(times, into.shape)


def kernel(
    n_row, n_col,
    a_tiles, a_blocks, a_count, b_tiles, b_blocks, b_count,
    coeff, bank_hbm, out,
    rows, cols, bank, a_fold, b_fold, a_mult, b_mult, local_sem, row_send, row_recv, col_send, col_recv,
):
    tile = coeff.shape[0]
    half = tile // 2
    n_bank = bank.shape[0]
    depth, width = n_row // 2, n_col // 2
    row, col = lax.axis_index("row"), lax.axis_index("col")
    z, y = row // 2, row % 2
    x, core = col // 2, col % 2
    mate = row + 1 - 2 * y
    twin = col + 1 - 2 * core

    def part(ref, which, h):
        return ref.at[which, pl.ds(h * half, half), :]

    def own(h):
        return coeff.at[pl.ds(h * half, half), :]

    def row_copy(src, which, h, way, target):
        return pltpu.make_async_remote_copy(
            src_ref=src, dst_ref=part(rows, which, h),
            send_sem=row_send.at[way, which, h], recv_sem=row_recv.at[which, h],
            device_id=(target, col), device_id_type=MESH,
        )

    def col_copy(src, which, h, way, target):
        return pltpu.make_async_remote_copy(
            src_ref=src, dst_ref=part(cols, which, h),
            send_sem=col_send.at[way, which, h], recv_sem=col_recv.at[which, h],
            device_id=(row, target), device_id_type=MESH,
        )

    def arrived(which, h):
        row_copy(own(h), which, h, 0, mate).wait_recv()

    bank_copy = pltpu.make_async_copy(bank_hbm, bank, local_sem.at[0])
    bank_copy.start()
    own_row = pltpu.make_async_copy(coeff, rows.at[row], local_sem.at[1])
    own_row.start()
    own_col = pltpu.make_async_copy(coeff, cols.at[col], local_sem.at[2])
    own_col.start()

    has_up, has_down = z + 1 < depth, z >= 1

    barrier = pltpu.get_barrier_semaphore()

    def greet(r, c):
        pl.semaphore_signal(barrier, inc=1, device_id=(r, c), device_id_type=MESH)

    @pl.when(has_up)
    def _():
        greet(row + 2, col)

    @pl.when(has_down)
    def _():
        greet(row - 2, col)

    greet(mate, col)
    greet(row, twin)
    for step in range(1, width):
        greet(row, lax.rem(x + step, width) * 2 + core)
    neighbours = 1 + width + has_up.astype(jnp.int32) + has_down.astype(jnp.int32)
    pl.semaphore_wait(barrier, neighbours)

    UP, DOWN, SIDE = 0, 1, 2

    for h in (0, 1):
        @pl.when(has_up)
        def _():
            row_copy(own(h), row, h, UP, row + 2).start()

        @pl.when(has_down)
        def _():
            row_copy(own(h), row, h, DOWN, row - 2).start()

        row_copy(own(h), row, h, SIDE, mate).start()
        for step in range(1, width):
            col_copy(own(h), col, h, step, lax.rem(x + step, width) * 2 + core).start()
        col_copy(own(h), col, h, 0, twin).start()

    def pass_rows(d, h):
        below, above = row - 2 * d, row + 2 * d

        @pl.when(z >= d)
        def _():
            arrived(below, h)

            @pl.when(has_up)
            def _():
                row_copy(part(rows, below, h), below, h, UP, row + 2).start()

            if d != 1 or h != LATE:
                row_copy(part(rows, below, h), below, h, SIDE, mate).start()

        @pl.when(z + d < depth)
        def _():
            arrived(above, h)

            @pl.when(has_down)
            def _():
                row_copy(part(rows, above, h), above, h, DOWN, row - 2).start()

            if d != 1 or h != LATE:
                row_copy(part(rows, above, h), above, h, SIDE, mate).start()

    def pass_mate():
        arrived(mate, LATE)

        @pl.when(has_up)
        def _():
            row_copy(part(rows, mate, LATE), mate, LATE, UP, row + 2).start()

        @pl.when(has_down)
        def _():
            row_copy(part(rows, mate, LATE), mate, LATE, DOWN, row - 2).start()

    def pass_cols(h):
        for step in range(1, width):
            source = lax.rem(x + width - step, width) * 2 + core
            col_copy(own(h), source, h, 0, twin).wait_recv()
            col_copy(part(cols, source, h), source, h, 0, twin).start()

    counted(a_tiles, a_blocks, row, a_count[row], n_bank, a_mult)
    counted(b_tiles, b_blocks, col, b_count[col], n_bank, b_mult)
    bank_copy.wait()

    def fold(mult, into, first, place, size):
        def body(chunk, carry):
            top = pl.multiple_of(chunk * STRIP, STRIP)
            totals = [None] * size
            for b in range(n_bank):
                block = bank[b, pl.ds(top, STRIP), :].astype(jnp.float32)
                for g in range(size):
                    term = mult[pl.ds((first + g) * n_bank + b, 1), :] * block
                    totals[g] = term if b == 0 else totals[g] + term
            for g in range(size):
                high = totals[g].astype(into.dtype)
                low = (totals[g] - high.astype(jnp.float32)).astype(into.dtype)
                into[place + g, pl.ds(top, STRIP), :] = high
                into[place + g, pl.ds(pl.multiple_of(tile + top, STRIP), STRIP), :] = low
            return carry

        lax.fori_loop(0, tile // STRIP, body, 0)

    def fold_rows(low, high):
        for first in range(low, high, GROUP):
            fold(a_mult, a_fold, first, first, min(GROUP, high - first))

    def add_row(which):
        both = jnp.dot(a_fold[which], rows[which], preferred_element_type=jnp.float32)
        out[...] += both[:tile] + both[tile:]

    def add_lane(base, d):
        def body(side, carry):
            which = base + (2 * side - 1) * 2 * d

            @pl.when(jnp.logical_and(which >= 0, which < n_row))
            def _():
                add_row(which)

            return carry

        lax.fori_loop(0, 2, body, 0)

    def await_lane(d):
        for h in (0, 1):
            @pl.when(z >= d)
            def _():
                arrived(mate - 2 * d, h)

            @pl.when(z + d < depth)
            def _():
                arrived(mate + 2 * d, h)

    out[...] = jnp.zeros_like(out)
    middle = n_row // 2
    fold_rows(0, middle)
    pass_rows(1, 0)
    pass_cols(0)
    fold_rows(middle, n_row)
    pass_rows(1, 1)
    pass_cols(1)
    own_col.wait()
    own_row.wait()

    for first in range(0, n_col, GROUP):
        size = min(GROUP, n_col - first)
        fold(b_mult, b_fold, first, 0, size)
        if first == 0:
            if depth > 2:
                pass_rows(2, 0)
            for h in (0, 1):
                for step in range(width):
                    source = lax.rem(x + step, width) * 2 + 1 - core
                    col_copy(own(h), source, h, 0, twin).wait_recv()

        def add_col(g, carry):
            both = lax.dot_general(
                cols[first + g], b_fold[g], (((1,), (1,)), ((), ())),
                preferred_element_type=jnp.float32,
            )
            out[...] += both[:, :tile] + both[:, tile:]
            return carry

        lax.fori_loop(0, size, add_col, 0)

    add_row(row)
    if depth > 2:
        pass_rows(2, 1)
    pass_mate()
    add_lane(row, 1)
    arrived(mate, 1 - LATE)
    add_row(mate)
    for d in range(3, depth):
        pass_rows(d, 0)
        if d == 3:
            add_lane(row, 2)
        pass_rows(d, 1)
    if depth == 3:
        add_lane(row, 2)
    for d in range(1, depth):
        await_lane(d)
        if d >= 3:
            add_lane(row, d)
        add_lane(mate, d)

    def sent_row(which, h, way):
        row_copy(own(h), which, h, way, mate).wait_send()

    for h in (0, 1):
        @pl.when(has_up)
        def _():
            sent_row(row, h, UP)

        @pl.when(has_down)
        def _():
            sent_row(row, h, DOWN)

        sent_row(row, h, SIDE)
        for step in range(1, width):
            col_copy(own(h), col, h, step, twin).wait_send()
        for step in range(width):
            source = lax.rem(x + step, width) * 2 + core
            col_copy(own(h), source, h, 0, twin).wait_send()
        for d in range(1, depth):
            @pl.when(z >= d)
            def _():
                @pl.when(has_up)
                def _():
                    sent_row(row - 2 * d, h, UP)

                if d != 1 or h != LATE:
                    sent_row(row - 2 * d, h, SIDE)

            @pl.when(z + d < depth)
            def _():
                @pl.when(has_down)
                def _():
                    sent_row(row + 2 * d, h, DOWN)

                if d != 1 or h != LATE:
                    sent_row(row + 2 * d, h, SIDE)

    @pl.when(has_up)
    def _():
        sent_row(mate, LATE, UP)

    @pl.when(has_down)
    def _():
        sent_row(mate, LATE, DOWN)


def solution(mesh):
    n_row, n_col = mesh.shape["row"], mesh.shape["col"]

    def local(coeff, bank, a_tiles, a_blocks, a_count, b_tiles, b_blocks, b_count):
        tile = coeff.shape[0]
        flops = 2 * (a_tiles.shape[1] + b_tiles.shape[1]) * tile**3
        return pl.pallas_call(
            functools.partial(kernel, n_row, n_col),
            out_shape=jax.ShapeDtypeStruct((tile, tile), jnp.float32),
            in_specs=([pl.BlockSpec(memory_space=pltpu.VMEM)] * 2 + [pl.BlockSpec(memory_space=pltpu.SMEM)]) * 2
            + [pl.BlockSpec(memory_space=pltpu.HBM)] * 2,
            out_specs=pl.BlockSpec(memory_space=pltpu.VMEM),
            scratch_shapes=[
                pltpu.VMEM((n_row, tile, tile), coeff.dtype),
                pltpu.VMEM((n_col, tile, tile), coeff.dtype),
                pltpu.VMEM(bank.shape, bank.dtype),
                pltpu.VMEM((n_row, 2 * tile, tile), bank.dtype),
                pltpu.VMEM((min(GROUP, n_col), 2 * tile, tile), bank.dtype),
                pltpu.VMEM((n_row * bank.shape[0], tile), jnp.float32),
                pltpu.VMEM((n_col * bank.shape[0], tile), jnp.float32),
                pltpu.SemaphoreType.DMA((3,)),
                pltpu.SemaphoreType.DMA((3, n_row, 2)),
                pltpu.SemaphoreType.DMA((n_row, 2)),
                pltpu.SemaphoreType.DMA((max(1, n_col // 2), n_col, 2)),
                pltpu.SemaphoreType.DMA((n_col, 2)),
            ],
            compiler_params=pltpu.CompilerParams(
                collective_id=0, has_side_effects=True, vmem_limit_bytes=62 * 1024 * 1024
            ),
            cost_estimate=pl.CostEstimate(
                flops=flops, bytes_accessed=bank.size * 2 + tile * tile * 6, transcendentals=0
            ),
        )(a_tiles, a_blocks, a_count, b_tiles, b_blocks, b_count, coeff, bank)

    return jax.shard_map(
        local,
        mesh=mesh,
        in_specs=(P("row", "col"), P(), P(), P(), P(), P(), P(), P()),
        out_specs=P("row", "col"),
        check_vma=False,
    )
```

```python
import functools

import jax
import jax.numpy as jnp
from jax import lax
from jax.experimental import pallas as pl
from jax.experimental.pallas import tpu as pltpu
from jax.sharding import PartitionSpec as P

MESH = pl.DeviceIdType.MESH
PARTS = 2
RELAY = (1,)


GROUP = 4
STRIP = 16


def counted(tiles, blocks, place, count, n_bank, into):
    code = tiles[pl.ds(place, 1), :] * n_bank + blocks[pl.ds(place, 1), :]
    slot = lax.broadcasted_iota(jnp.int32, code.shape, 1)
    code = jnp.where(slot < count, code, -1)
    shape = (into.shape[0], code.shape[1])
    hit = lax.broadcasted_iota(jnp.int32, shape, 0) == code
    times = jnp.sum(jnp.where(hit, 1.0, 0.0).astype(jnp.float32), axis=1, keepdims=True)
    into[...] = jnp.broadcast_to(times, into.shape)


def kernel(
    n_row, n_col,
    a_tiles, a_blocks, a_count, b_tiles, b_blocks, b_count,
    coeff, bank_hbm, out, beta_hbm,
    rows, cols, bank, a_fold, b_fold, a_mult, b_mult, beta, local_sem, row_send, row_recv, col_send, col_recv,
):
    tile = coeff.shape[0]
    half = tile // PARTS
    n_bank = bank.shape[0]
    depth, width = n_row // 2, n_col // 2
    row, col = lax.axis_index("row"), lax.axis_index("col")
    z, y = row // 2, row % 2
    x, core = col // 2, col % 2
    mate = row + 1 - 2 * y
    twin = col + 1 - 2 * core

    def part(ref, which, h):
        return ref.at[which, pl.ds(h * half, half), :]

    def own(h):
        return coeff.at[pl.ds(h * half, half), :]

    def row_copy(src, which, h, way, target):
        return pltpu.make_async_remote_copy(
            src_ref=src, dst_ref=part(rows, which, h),
            send_sem=row_send.at[way, which, h], recv_sem=row_recv.at[which, h],
            device_id=(target, col), device_id_type=MESH,
        )

    def col_copy(src, which, h, way, target):
        return pltpu.make_async_remote_copy(
            src_ref=src, dst_ref=part(cols, which, h),
            send_sem=col_send.at[way, which, h], recv_sem=col_recv.at[which, h],
            device_id=(row, target), device_id_type=MESH,
        )

    def arrived(which, h):
        row_copy(own(h), which, h, 0, mate).wait_recv()

    bank_copy = pltpu.make_async_copy(bank_hbm, bank, local_sem.at[0])
    bank_copy.start()
    own_row = pltpu.make_async_copy(coeff, rows.at[row], local_sem.at[1])
    own_row.start()
    own_col = pltpu.make_async_copy(coeff, cols.at[col], local_sem.at[2])
    own_col.start()

    has_up, has_down = z + 1 < depth, z >= 1

    barrier = pltpu.get_barrier_semaphore()

    def greet(r, c):
        pl.semaphore_signal(barrier, inc=1, device_id=(r, c), device_id_type=MESH)

    @pl.when(has_up)
    def _():
        greet(row + 2, col)

    @pl.when(has_down)
    def _():
        greet(row - 2, col)

    greet(mate, col)
    greet(row, twin)
    for step in range(1, width):
        greet(row, lax.rem(x + step, width) * 2 + core)
    neighbours = 1 + width + has_up.astype(jnp.int32) + has_down.astype(jnp.int32)
    pl.semaphore_wait(barrier, neighbours)

    UP, DOWN, SIDE = 0, 1, 2

    for h in range(PARTS):
        @pl.when(has_up)
        def _():
            row_copy(own(h), row, h, UP, row + 2).start()

        @pl.when(has_down)
        def _():
            row_copy(own(h), row, h, DOWN, row - 2).start()

        row_copy(own(h), row, h, SIDE, mate).start()
        for step in range(1, width):
            col_copy(own(h), col, h, step, lax.rem(x + step, width) * 2 + core).start()
        col_copy(own(h), col, h, 0, twin).start()

    chained = depth > 2

    def to_mate(which, d, h, beside_end):
        if chained and d == depth - 1 and h in RELAY:
            return

        def go():
            row_copy(part(rows, which, h), which, h, SIDE, mate).start()

        if chained and d == 1:
            pl.when(jnp.logical_not(beside_end))(go)
        else:
            go()

    def pass_rows(d, h):
        below, above = row - 2 * d, row + 2 * d

        @pl.when(z >= d)
        def _():
            arrived(below, h)

            @pl.when(has_up)
            def _():
                row_copy(part(rows, below, h), below, h, UP, row + 2).start()

            to_mate(below, d, h, z == 1)

        @pl.when(z + d < depth)
        def _():
            arrived(above, h)

            @pl.when(has_down)
            def _():
                row_copy(part(rows, above, h), above, h, DOWN, row - 2).start()

            to_mate(above, d, h, z == depth - 2)

    def pass_mate(h):
        if not chained:
            return

        @pl.when(z == 0)
        def _():
            arrived(mate, h)
            row_copy(part(rows, mate, h), mate, h, UP, row + 2).start()

        @pl.when(z == depth - 1)
        def _():
            arrived(mate, h)
            row_copy(part(rows, mate, h), mate, h, DOWN, row - 2).start()

    far_high, far_low = mate + 2 * (depth - 1 - z), mate - 2 * z

    def relay(h):
        if not chained:
            return

        @pl.when(z == 1)
        def _():
            arrived(far_high, h)
            row_copy(part(rows, far_high, h), far_high, h, DOWN, row - 2).start()

        @pl.when(z == depth - 2)
        def _():
            arrived(far_low, h)
            row_copy(part(rows, far_low, h), far_low, h, UP, row + 2).start()

    def pass_cols(h):
        for step in range(1, width):
            source = lax.rem(x + width - step, width) * 2 + core
            col_copy(own(h), source, h, 0, twin).wait_recv()
            col_copy(part(cols, source, h), source, h, 0, twin).start()

    counted(a_tiles, a_blocks, row, a_count[row], n_bank, a_mult)
    counted(b_tiles, b_blocks, col, b_count[col], n_bank, b_mult)
    bank_copy.wait()

    def fold(mult, into, first, place, size):
        def body(chunk, carry):
            top = pl.multiple_of(chunk * STRIP, STRIP)
            totals = [None] * size
            for b in range(n_bank):
                block = bank[b, pl.ds(top, STRIP), :].astype(jnp.float32)
                for g in range(size):
                    term = mult[pl.ds((first + g) * n_bank + b, 1), :] * block
                    totals[g] = term if b == 0 else totals[g] + term
            for g in range(size):
                high = totals[g].astype(into.dtype)
                low = (totals[g] - high.astype(jnp.float32)).astype(into.dtype)
                into[place + g, pl.ds(top, STRIP), :] = high
                into[place + g, pl.ds(pl.multiple_of(tile + top, STRIP), STRIP), :] = low
            return carry

        lax.fori_loop(0, tile // STRIP, body, 0)

    def fold_rows(low, high):
        for first in range(low, high, GROUP):
            fold(a_mult, a_fold, first, first, min(GROUP, high - first))

    def add_row(which):
        both = jnp.dot(a_fold[which], rows[which], preferred_element_type=jnp.float32)
        out[...] += both[:tile] + both[tile:]

    def add_lane(base, d):
        def body(side, carry):
            which = base + (2 * side - 1) * 2 * d

            @pl.when(jnp.logical_and(which >= 0, which < n_row))
            def _():
                add_row(which)

            return carry

        lax.fori_loop(0, 2, body, 0)

    def await_mate(d):
        for h in range(PARTS):
            if chained and h in RELAY:
                if d == 0:
                    @pl.when(jnp.logical_and(z > 0, z < depth - 1))
                    def _():
                        arrived(mate, h)
                    continue
                if d == depth - 2:
                    @pl.when(jnp.logical_and(z >= d, z != depth - 2))
                    def _():
                        arrived(mate - 2 * d, h)

                    @pl.when(jnp.logical_and(z + d < depth, z != 1))
                    def _():
                        arrived(mate + 2 * d, h)
                    continue
            if d == 0:
                if chained:
                    @pl.when(jnp.logical_and(z > 0, z < depth - 1))
                    def _():
                        arrived(mate, h)
                else:
                    arrived(mate, h)
                continue

            @pl.when(z >= d)
            def _():
                arrived(mate - 2 * d, h)

            @pl.when(z + d < depth)
            def _():
                arrived(mate + 2 * d, h)

    out[...] = jnp.zeros_like(out)
    beta[...] = jnp.zeros_like(beta)
    middle = n_row // 2
    fold_rows(0, middle)
    for h in range(PARTS // 2):
        if depth > 1:
            pass_rows(1, h)
        pass_mate(h)
        pass_cols(h)
    fold_rows(middle, n_row)
    for h in range(PARTS // 2, PARTS):
        if depth > 1:
            pass_rows(1, h)
        pass_mate(h)
        pass_cols(h)
    own_col.wait()
    own_row.wait()

    for first in range(0, n_col, GROUP):
        size = min(GROUP, n_col - first)
        fold(b_mult, b_fold, first, 0, size)
        if first == 0:
            if depth > 3:
                for h in range(PARTS // 2):
                    pass_rows(2, h)
            for h in range(PARTS):
                for step in range(width):
                    source = lax.rem(x + step, width) * 2 + 1 - core
                    col_copy(own(h), source, h, 0, twin).wait_recv()

        def add_col(g, carry):
            both = lax.dot_general(
                cols[first + g], b_fold[g], (((1,), (1,)), ((), ())),
                preferred_element_type=jnp.float32,
            )
            beta[...] += both[:, :tile] + both[:, tile:]
            return carry

        lax.fori_loop(0, size, add_col, 0)

    beta_copy = pltpu.make_async_copy(beta, beta_hbm, local_sem.at[3])
    beta_copy.start()
    add_row(row)
    if depth > 3:
        for h in range(PARTS // 2, PARTS):
            pass_rows(2, h)
    if depth > 1:
        add_lane(row, 1)
    await_mate(0)
    add_row(mate)
    for d in range(3, depth - 1):
        for h in range(PARTS):
            pass_rows(d, h)
    for h in RELAY:
        relay(h)
    if depth > 2:
        for h in range(PARTS // 2):
            pass_rows(depth - 1, h)
        if depth > 3:
            add_lane(row, 2)
        for h in range(PARTS // 2, PARTS):
            pass_rows(depth - 1, h)
    for d in range(1, depth):
        if d == depth - 1 and d > 1 or d > 2:
            add_lane(row, d)
        await_mate(d)
        add_lane(mate, d)

    beta_copy.wait()
    def sent_row(which, h, way):
        row_copy(own(h), which, h, way, mate).wait_send()

    for h in range(PARTS):
        @pl.when(has_up)
        def _():
            sent_row(row, h, UP)

        @pl.when(has_down)
        def _():
            sent_row(row, h, DOWN)

        sent_row(row, h, SIDE)
        for step in range(1, width):
            col_copy(own(h), col, h, step, twin).wait_send()
        for step in range(width):
            source = lax.rem(x + step, width) * 2 + core
            col_copy(own(h), source, h, 0, twin).wait_send()
        for d in range(1, depth):
            def left_for_mate(which, beside_end):
                if chained and d == depth - 1 and h in RELAY:
                    return
                if chained and d == 1:
                    pl.when(jnp.logical_not(beside_end))(lambda: sent_row(which, h, SIDE))
                else:
                    sent_row(which, h, SIDE)

            @pl.when(z >= d)
            def _():
                @pl.when(has_up)
                def _():
                    sent_row(row - 2 * d, h, UP)

                left_for_mate(row - 2 * d, z == 1)

            @pl.when(z + d < depth)
            def _():
                @pl.when(has_down)
                def _():
                    sent_row(row + 2 * d, h, DOWN)

                left_for_mate(row + 2 * d, z == depth - 2)

    if chained:
        @pl.when(z == 0)
        def _():
            for h in range(PARTS):
                sent_row(mate, h, UP)

        @pl.when(z == depth - 1)
        def _():
            for h in range(PARTS):
                sent_row(mate, h, DOWN)

        @pl.when(z == 1)
        def _():
            for h in RELAY:
                sent_row(far_high, h, DOWN)

        @pl.when(z == depth - 2)
        def _():
            for h in RELAY:
                sent_row(far_low, h, UP)


def solution(mesh):
    n_row, n_col = mesh.shape["row"], mesh.shape["col"]

    def local(coeff, bank, a_tiles, a_blocks, a_count, b_tiles, b_blocks, b_count):
        tile = coeff.shape[0]
        flops = 2 * (a_tiles.shape[1] + b_tiles.shape[1]) * tile**3
        sigma_alpha, sigma_beta = pl.pallas_call(
            functools.partial(kernel, n_row, n_col),
            out_shape=[jax.ShapeDtypeStruct((tile, tile), jnp.float32)] * 2,
            in_specs=([pl.BlockSpec(memory_space=pltpu.VMEM)] * 2 + [pl.BlockSpec(memory_space=pltpu.SMEM)]) * 2
            + [pl.BlockSpec(memory_space=pltpu.HBM)] * 2,
            out_specs=[pl.BlockSpec(memory_space=pltpu.VMEM), pl.BlockSpec(memory_space=pltpu.HBM)],
            scratch_shapes=[
                pltpu.VMEM((n_row, tile, tile), coeff.dtype),
                pltpu.VMEM((n_col, tile, tile), coeff.dtype),
                pltpu.VMEM(bank.shape, bank.dtype),
                pltpu.VMEM((n_row, 2 * tile, tile), bank.dtype),
                pltpu.VMEM((min(GROUP, n_col), 2 * tile, tile), bank.dtype),
                pltpu.VMEM((n_row * bank.shape[0], tile), jnp.float32),
                pltpu.VMEM((n_col * bank.shape[0], tile), jnp.float32),
                pltpu.VMEM((tile, tile), jnp.float32),
                pltpu.SemaphoreType.DMA((4,)),
                pltpu.SemaphoreType.DMA((3, n_row, PARTS)),
                pltpu.SemaphoreType.DMA((n_row, PARTS)),
                pltpu.SemaphoreType.DMA((max(1, n_col // 2), n_col, PARTS)),
                pltpu.SemaphoreType.DMA((n_col, PARTS)),
            ],
            compiler_params=pltpu.CompilerParams(
                collective_id=0, has_side_effects=True, vmem_limit_bytes=62 * 1024 * 1024
            ),
            cost_estimate=pl.CostEstimate(
                flops=flops, bytes_accessed=bank.size * 2 + tile * tile * 6, transcendentals=0
            ),
        )(a_tiles, a_blocks, a_count, b_tiles, b_blocks, b_count, coeff, bank)
        return sigma_alpha + sigma_beta

    return jax.shard_map(
        local,
        mesh=mesh,
        in_specs=(P("row", "col"), P(), P(), P(), P(), P(), P(), P()),
        out_specs=P("row", "col"),
        check_vma=False,
    )
```

```python
import functools

import jax
import jax.numpy as jnp
from jax import lax
from jax.experimental import pallas as pl
from jax.experimental.pallas import tpu as pltpu
from jax.sharding import PartitionSpec as P

MESH = pl.DeviceIdType.MESH
PARTS = 2
RELAY = (1,)


GROUP = 4
STRIP = 16


def counted(tiles, blocks, place, count, n_bank, into):
    code = tiles[pl.ds(place, 1), :] * n_bank + blocks[pl.ds(place, 1), :]
    slot = lax.broadcasted_iota(jnp.int32, code.shape, 1)
    code = jnp.where(slot < count, code, -1)
    shape = (into.shape[0], code.shape[1])
    hit = lax.broadcasted_iota(jnp.int32, shape, 0) == code
    times = jnp.sum(jnp.where(hit, 1.0, 0.0).astype(jnp.float32), axis=1, keepdims=True)
    into[...] = jnp.broadcast_to(times, into.shape)


def kernel(
    n_row, n_col,
    a_tiles, a_blocks, a_count, b_tiles, b_blocks, b_count,
    coeff, bank_hbm, out,
    rows, cols, bank, a_fold, b_fold, a_mult, b_mult, local_sem, row_send, row_recv, col_send, col_recv,
):
    tile = coeff.shape[0]
    half = tile // PARTS
    n_bank = bank.shape[0]
    depth, width = n_row // 2, n_col // 2
    row, col = lax.axis_index("row"), lax.axis_index("col")
    z, y = row // 2, row % 2
    x, core = col // 2, col % 2
    mate = row + 1 - 2 * y
    twin = col + 1 - 2 * core

    def part(ref, which, h):
        return ref.at[which, pl.ds(h * half, half), :]

    def own(h):
        return coeff.at[pl.ds(h * half, half), :]

    def row_copy(src, which, h, way, target):
        return pltpu.make_async_remote_copy(
            src_ref=src, dst_ref=part(rows, which, h),
            send_sem=row_send.at[way, which, h], recv_sem=row_recv.at[which, h],
            device_id=(target, col), device_id_type=MESH,
        )

    def col_copy(src, which, h, way, target):
        return pltpu.make_async_remote_copy(
            src_ref=src, dst_ref=part(cols, which, h),
            send_sem=col_send.at[way, which, h], recv_sem=col_recv.at[which, h],
            device_id=(row, target), device_id_type=MESH,
        )

    def arrived(which, h):
        row_copy(own(h), which, h, 0, mate).wait_recv()

    bank_copy = pltpu.make_async_copy(bank_hbm, bank, local_sem.at[0])
    bank_copy.start()
    own_row = pltpu.make_async_copy(coeff, rows.at[row], local_sem.at[1])
    own_row.start()
    own_col = pltpu.make_async_copy(coeff, cols.at[col], local_sem.at[2])
    own_col.start()

    has_up, has_down = z + 1 < depth, z >= 1

    barrier = pltpu.get_barrier_semaphore()

    def greet(r, c):
        pl.semaphore_signal(barrier, inc=1, device_id=(r, c), device_id_type=MESH)

    @pl.when(has_up)
    def _():
        greet(row + 2, col)

    @pl.when(has_down)
    def _():
        greet(row - 2, col)

    greet(mate, col)
    greet(row, twin)
    for step in range(1, width):
        greet(row, lax.rem(x + step, width) * 2 + core)
    neighbours = 1 + width + has_up.astype(jnp.int32) + has_down.astype(jnp.int32)
    pl.semaphore_wait(barrier, neighbours)

    UP, DOWN, SIDE = 0, 1, 2

    for h in range(PARTS):
        @pl.when(has_up)
        def _():
            row_copy(own(h), row, h, UP, row + 2).start()

        @pl.when(has_down)
        def _():
            row_copy(own(h), row, h, DOWN, row - 2).start()

        row_copy(own(h), row, h, SIDE, mate).start()
        for step in range(1, width):
            col_copy(own(h), col, h, step, lax.rem(x + step, width) * 2 + core).start()
        col_copy(own(h), col, h, 0, twin).start()

    chained = depth > 2

    def to_mate(which, d, h, beside_end):
        if chained and d == depth - 1 and h in RELAY:
            return

        def go():
            row_copy(part(rows, which, h), which, h, SIDE, mate).start()

        if chained and d == 1:
            pl.when(jnp.logical_not(beside_end))(go)
        else:
            go()

    def pass_rows(d, h):
        below, above = row - 2 * d, row + 2 * d

        @pl.when(z >= d)
        def _():
            arrived(below, h)

            @pl.when(has_up)
            def _():
                row_copy(part(rows, below, h), below, h, UP, row + 2).start()

            to_mate(below, d, h, z == 1)

        @pl.when(z + d < depth)
        def _():
            arrived(above, h)

            @pl.when(has_down)
            def _():
                row_copy(part(rows, above, h), above, h, DOWN, row - 2).start()

            to_mate(above, d, h, z == depth - 2)

    def pass_mate(h):
        if not chained:
            return

        @pl.when(z == 0)
        def _():
            arrived(mate, h)
            row_copy(part(rows, mate, h), mate, h, UP, row + 2).start()

        @pl.when(z == depth - 1)
        def _():
            arrived(mate, h)
            row_copy(part(rows, mate, h), mate, h, DOWN, row - 2).start()

    far_high, far_low = mate + 2 * (depth - 1 - z), mate - 2 * z

    def relay(h):
        if not chained:
            return

        @pl.when(z == 1)
        def _():
            arrived(far_high, h)
            row_copy(part(rows, far_high, h), far_high, h, DOWN, row - 2).start()

        @pl.when(z == depth - 2)
        def _():
            arrived(far_low, h)
            row_copy(part(rows, far_low, h), far_low, h, UP, row + 2).start()

    def pass_cols(h):
        for step in range(1, width):
            source = lax.rem(x + width - step, width) * 2 + core
            col_copy(own(h), source, h, 0, twin).wait_recv()
            col_copy(part(cols, source, h), source, h, 0, twin).start()

    counted(a_tiles, a_blocks, row, a_count[row], n_bank, a_mult)
    counted(b_tiles, b_blocks, col, b_count[col], n_bank, b_mult)
    bank_copy.wait()

    def fold(mult, into, first, place, size):
        def body(chunk, carry):
            top = pl.multiple_of(chunk * STRIP, STRIP)
            totals = [None] * size
            for b in range(n_bank):
                block = bank[b, pl.ds(top, STRIP), :].astype(jnp.float32)
                for g in range(size):
                    term = mult[pl.ds((first + g) * n_bank + b, 1), :] * block
                    totals[g] = term if b == 0 else totals[g] + term
            for g in range(size):
                high = totals[g].astype(into.dtype)
                low = (totals[g] - high.astype(jnp.float32)).astype(into.dtype)
                into[place + g, pl.ds(top, STRIP), :] = high
                into[place + g, pl.ds(pl.multiple_of(tile + top, STRIP), STRIP), :] = low
            return carry

        lax.fori_loop(0, tile // STRIP, body, 0)

    def fold_rows(low, high):
        for first in range(low, high, GROUP):
            fold(a_mult, a_fold, first, first, min(GROUP, high - first))

    def add_row(which):
        both = jnp.dot(a_fold[which], rows[which], preferred_element_type=jnp.float32)
        out[...] += both[:tile] + both[tile:]

    def add_lane(base, d):
        def body(side, carry):
            which = base + (2 * side - 1) * 2 * d

            @pl.when(jnp.logical_and(which >= 0, which < n_row))
            def _():
                add_row(which)

            return carry

        lax.fori_loop(0, 2, body, 0)

    def await_mate(d):
        for h in range(PARTS):
            if chained and h in RELAY:
                if d == 0:
                    @pl.when(jnp.logical_and(z > 0, z < depth - 1))
                    def _():
                        arrived(mate, h)
                    continue
                if d == depth - 2:
                    @pl.when(jnp.logical_and(z >= d, z != depth - 2))
                    def _():
                        arrived(mate - 2 * d, h)

                    @pl.when(jnp.logical_and(z + d < depth, z != 1))
                    def _():
                        arrived(mate + 2 * d, h)
                    continue
            if d == 0:
                if chained:
                    @pl.when(jnp.logical_and(z > 0, z < depth - 1))
                    def _():
                        arrived(mate, h)
                else:
                    arrived(mate, h)
                continue

            @pl.when(z >= d)
            def _():
                arrived(mate - 2 * d, h)

            @pl.when(z + d < depth)
            def _():
                arrived(mate + 2 * d, h)

    out[...] = jnp.zeros_like(out)
    middle = n_row // 2
    fold_rows(0, middle)
    for h in range(PARTS // 2):
        if depth > 1:
            pass_rows(1, h)
        pass_mate(h)
        pass_cols(h)
    fold_rows(middle, n_row)
    for h in range(PARTS // 2, PARTS):
        if depth > 1:
            pass_rows(1, h)
        pass_mate(h)
        pass_cols(h)
    own_col.wait()
    own_row.wait()

    for first in range(0, n_col, GROUP):
        size = min(GROUP, n_col - first)
        fold(b_mult, b_fold, first, 0, size)
        if first == 0:
            if depth > 3:
                for h in range(PARTS // 2):
                    pass_rows(2, h)
            for h in range(PARTS):
                for step in range(width):
                    source = lax.rem(x + step, width) * 2 + 1 - core
                    col_copy(own(h), source, h, 0, twin).wait_recv()

        def add_col(g, carry):
            both = lax.dot_general(
                cols[first + g], b_fold[g], (((1,), (1,)), ((), ())),
                preferred_element_type=jnp.float32,
            )
            out[...] += both[:, :tile] + both[:, tile:]
            return carry

        lax.fori_loop(0, size, add_col, 0)

    add_row(row)
    if depth > 3:
        for h in range(PARTS // 2, PARTS):
            pass_rows(2, h)
    if depth > 1:
        add_lane(row, 1)
    await_mate(0)
    add_row(mate)
    for d in range(3, depth - 1):
        for h in range(PARTS):
            pass_rows(d, h)
    for h in RELAY:
        relay(h)
    if depth > 2:
        for h in range(PARTS // 2):
            pass_rows(depth - 1, h)
        if depth > 3:
            add_lane(row, 2)
        for h in range(PARTS // 2, PARTS):
            pass_rows(depth - 1, h)
    for d in range(1, depth):
        if d == depth - 1 and d > 1 or d > 2:
            add_lane(row, d)
        await_mate(d)
        add_lane(mate, d)

    def sent_row(which, h, way):
        row_copy(own(h), which, h, way, mate).wait_send()

    for h in range(PARTS):
        @pl.when(has_up)
        def _():
            sent_row(row, h, UP)

        @pl.when(has_down)
        def _():
            sent_row(row, h, DOWN)

        sent_row(row, h, SIDE)
        for step in range(1, width):
            col_copy(own(h), col, h, step, twin).wait_send()
        for step in range(width):
            source = lax.rem(x + step, width) * 2 + core
            col_copy(own(h), source, h, 0, twin).wait_send()
        for d in range(1, depth):
            def left_for_mate(which, beside_end):
                if chained and d == depth - 1 and h in RELAY:
                    return
                if chained and d == 1:
                    pl.when(jnp.logical_not(beside_end))(lambda: sent_row(which, h, SIDE))
                else:
                    sent_row(which, h, SIDE)

            @pl.when(z >= d)
            def _():
                @pl.when(has_up)
                def _():
                    sent_row(row - 2 * d, h, UP)

                left_for_mate(row - 2 * d, z == 1)

            @pl.when(z + d < depth)
            def _():
                @pl.when(has_down)
                def _():
                    sent_row(row + 2 * d, h, DOWN)

                left_for_mate(row + 2 * d, z == depth - 2)

    if chained:
        @pl.when(z == 0)
        def _():
            for h in range(PARTS):
                sent_row(mate, h, UP)

        @pl.when(z == depth - 1)
        def _():
            for h in range(PARTS):
                sent_row(mate, h, DOWN)

        @pl.when(z == 1)
        def _():
            for h in RELAY:
                sent_row(far_high, h, DOWN)

        @pl.when(z == depth - 2)
        def _():
            for h in RELAY:
                sent_row(far_low, h, UP)


def solution(mesh):
    n_row, n_col = mesh.shape["row"], mesh.shape["col"]

    def local(coeff, bank, a_tiles, a_blocks, a_count, b_tiles, b_blocks, b_count):
        tile = coeff.shape[0]
        flops = 2 * (a_tiles.shape[1] + b_tiles.shape[1]) * tile**3
        return pl.pallas_call(
            functools.partial(kernel, n_row, n_col),
            out_shape=jax.ShapeDtypeStruct((tile, tile), jnp.float32),
            in_specs=([pl.BlockSpec(memory_space=pltpu.VMEM)] * 2 + [pl.BlockSpec(memory_space=pltpu.SMEM)]) * 2
            + [pl.BlockSpec(memory_space=pltpu.HBM)] * 2,
            out_specs=pl.BlockSpec(memory_space=pltpu.VMEM),
            scratch_shapes=[
                pltpu.VMEM((n_row, tile, tile), coeff.dtype),
                pltpu.VMEM((n_col, tile, tile), coeff.dtype),
                pltpu.VMEM(bank.shape, bank.dtype),
                pltpu.VMEM((n_row, 2 * tile, tile), bank.dtype),
                pltpu.VMEM((min(GROUP, n_col), 2 * tile, tile), bank.dtype),
                pltpu.VMEM((n_row * bank.shape[0], tile), jnp.float32),
                pltpu.VMEM((n_col * bank.shape[0], tile), jnp.float32),
                pltpu.SemaphoreType.DMA((3,)),
                pltpu.SemaphoreType.DMA((3, n_row, PARTS)),
                pltpu.SemaphoreType.DMA((n_row, PARTS)),
                pltpu.SemaphoreType.DMA((max(1, n_col // 2), n_col, PARTS)),
                pltpu.SemaphoreType.DMA((n_col, PARTS)),
            ],
            compiler_params=pltpu.CompilerParams(
                collective_id=0, has_side_effects=True, vmem_limit_bytes=62 * 1024 * 1024
            ),
            cost_estimate=pl.CostEstimate(
                flops=flops, bytes_accessed=bank.size * 2 + tile * tile * 6, transcendentals=0
            ),
        )(a_tiles, a_blocks, a_count, b_tiles, b_blocks, b_count, coeff, bank)

    return jax.shard_map(
        local,
        mesh=mesh,
        in_specs=(P("row", "col"), P(), P(), P(), P(), P(), P(), P()),
        out_specs=P("row", "col"),
        check_vma=False,
    )
```
